128 devices in a mesh: rows: 32 (over z, x, core), cols: 4 (over y).
Axes of the slice: x: 4, y: 4, z: 4, core: 2. Of those that a mesh axis runs over, the one named last changes fastest.
Arguments:
- panel_cols: float32 [262144, 256], P(('rows', 'cols')), may hold values from -10000 to 10000, as said below
- trailing: float32 [262144, 1024], P('rows', 'cols'), may hold values from -200000 to 200000
Outputs:
- r_factor: float32 [256, 256], replicated
- r_cross: float32 [256, 1024], P(None, 'cols')
- updated: float32 [262144, 1024], P('rows', 'cols')
The draws below stay inside these ranges and needn't reach their ends.
Inputs may be any that keep to these rules, and one draw needn't show every extreme that they name: panel_cols has full column rank.
All inputs are finite; a program needn't handle non-finite values.
Results may differ from the reference program's by a relative error of at most 0.0003.
Values sent between devices are 32-bit elements; how exact they have to be, the bound alone decides.
No kernel may reach another device: no remote copies, remote signals or barrier semaphores. Data moves between devices by JAX's collectives and lax.ppermute only.
A program may use at most 128 MiB of HBM per device.

```python
import math
import jax
import jax.numpy as jnp
from jax import lax

B = 256
NC = 1024
ROWS = 262144


def panel_matrix(key):
    keys = jax.random.split(jax.random.fold_in(key, 11), 4)
    position = jnp.arange(ROWS, dtype=jnp.float32) / ROWS
    base_entries = jnp.clip(jax.random.normal(keys[0], (ROWS, B), jnp.float32), -6.0, 6.0)
    spread = jax.random.uniform(keys[1], (ROWS, 1), jnp.float32, 0.0, 1.0)
    row_scale = jnp.power(10.0, spread) * jnp.power(3.0, 0.5 * position)[:, None] / 6.0
    column_scale = jnp.exp(jax.random.uniform(keys[2], (B,), jnp.float32, 0.0, math.log(10.0)))
    perturb = jnp.clip(jax.random.normal(keys[3], (B, B), jnp.float32), -6.0, 6.0) * (0.35 / math.sqrt(B))
    mixing = (jnp.eye(B, dtype=jnp.float32) + perturb) * column_scale[None, :]
    return jnp.dot(base_entries * row_scale, mixing, precision=lax.Precision.HIGHEST)


def draw_panel_cols(key, part):
    return panel_matrix(key)


def draw_trailing(key, part):
    matrix = panel_matrix(key)
    keys = jax.random.split(jax.random.fold_in(key, 23), 2)
    coeffs = jnp.clip(jax.random.normal(keys[0], (B, NC), jnp.float32), -6.0, 6.0) * (0.6 / (4.6 * math.sqrt(B)))
    noise = jnp.clip(jax.random.normal(keys[1], (ROWS, NC), jnp.float32), -6.0, 6.0)
    return jnp.dot(matrix, coeffs, precision=lax.Precision.HIGHEST) + noise


def setup_inputs(seed: int = 0) -> dict:
    splits = jax.random.split(jax.random.key(seed), 3)
    return {
        "panel_cols": draw_panel_cols(jax.random.fold_in(splits[2], 71), 0),
        "trailing": draw_trailing(jax.random.fold_in(splits[2], 71), 0),
    }


def reference(panel_cols, trailing):
    orthonormal, upper_factor = jnp.linalg.qr(panel_cols, mode='reduced')
    sign_flip = jnp.where(jnp.diagonal(upper_factor) < 0, -1.0, 1.0).astype(upper_factor.dtype)
    upper_factor = upper_factor * sign_flip[:, None]
    orthonormal = orthonormal * sign_flip[None, :]
    coupling = jnp.dot(orthonormal.T, trailing, precision=lax.Precision.HIGHEST)
    updated = trailing - jnp.dot(orthonormal, coupling, precision=lax.Precision.HIGHEST)
    shrink = 1.0 / math.sqrt(ROWS)
    return (upper_factor * shrink, coupling * shrink, updated)
```

```python
import math

import jax
import jax.numpy as jnp
from jax import lax
from jax.experimental import pallas as pl
from jax.experimental.pallas import tpu as pltpu
from jax.sharding import PartitionSpec as P

F32, BF16 = jnp.float32, jnp.bfloat16
HIGHEST = lax.Precision.HIGHEST
BLOCK = 512


def over_rows(move):
    pairs = []
    for z in range(4):
        for x in range(4):
            for core in range(2):
                z2, x2, core2 = move(z, x, core)
                pairs.append(((z * 4 + x) * 2 + core, (z2 % 4 * 4 + x2 % 4) * 2 + core2))
    return pairs


PARTNER = over_rows(lambda z, x, core: (z, x, 1 - core))
FIRST = [over_rows(lambda z, x, core, k=k: (z, x + k, core) if core == 0 else (z + k, x, core)) for k in (2, 1, 3)]
SECOND = [over_rows(lambda z, x, core, k=k: (z + k, x, core) if core == 0 else (z, x + k, core)) for k in (2, 1, 3)]


def around(k):
    return [(i, (i + k) % 4) for i in range(4)]


def exchange_sum(part, axis, moves):
    others = [lax.ppermute(part, axis, move) for move in moves]
    return part + others[0] + others[1] + others[2]


def halves(part, core):
    half = part.shape[0] // 2
    keep = lax.dynamic_slice_in_dim(part, core * half, half)
    send = lax.dynamic_slice_in_dim(part, (1 - core) * half, half)
    return keep + lax.ppermute(send, "rows", PARTNER)


def joined(mine, core):
    other = lax.ppermute(mine, "rows", PARTNER)
    return jnp.where(core == 0, jnp.concatenate([mine, other]), jnp.concatenate([other, mine]))


def inner(left, right, precision):
    return lax.dot_general(left, right, (((0,), (0,)), ((), ())), precision=precision)


def split(value):
    high = value.astype(BF16)
    return high, (value - high.astype(F32)).astype(BF16)


def matmul3(left, right):
    (left_high, left_low), (right_high, right_low) = left, right
    dot = lambda a, b: jnp.dot(a, b, preferred_element_type=F32)
    return dot(left_high, right_high) + dot(left_low, right_high) + dot(left_high, right_low)


def update_kernel(shrink, place, cross, inverse, own, la, lb, ra, rb, oa, ob, trailing, updated, r_cross, w_high, w_low):
    step = pl.program_id(0)

    @pl.when(step == 0)
    def _():
        coupling = jnp.dot(inverse[...], cross[...], precision=HIGHEST, preferred_element_type=F32)
        r_cross[...] = coupling * shrink
        weights = lax.dot_general(inverse[...], coupling, (((0,), (0,)), ((), ())), precision=HIGHEST, preferred_element_type=F32)
        w_high[...], w_low[...] = split(weights)

    per = 1024 // BLOCK
    first = 0
    for piece in (own, la, lb, ra, rb, oa, ob):
        count = 2 * per if piece is own else per

        @pl.when((step >= first) & (step < first + count))
        def _(piece=piece):
            product = matmul3(split(piece[...]), (w_high[...], w_low[...]))
            updated[...] = trailing[...] - product

        first += count


def update(cross, inverse, pieces, trailing, place, shrink):
    per = 1024 // BLOCK
    full = pl.BlockSpec((256, 256), lambda i, place: (0, 0))
    specs, first = [], 0
    for piece in pieces:
        count = piece.shape[0] // BLOCK
        specs.append(pl.BlockSpec((BLOCK, 256), lambda i, place, first=first, count=count: (jnp.clip(i - first, 0, count - 1), 0)))
        first += count
    chunk = 2 * per

    def row(i, place):
        which = i // chunk
        offset = jnp.where(which == 0, 0, jnp.where(which == 1, 3, jnp.where(which == 2, 1, 2)))
        return ((place[0] + offset) % 4 * chunk + i % chunk, 0)

    wide = pl.BlockSpec((BLOCK, 256), row)
    return pl.pallas_call(
        lambda *refs: update_kernel(shrink, *refs),
        out_shape=[jax.ShapeDtypeStruct(trailing.shape, F32), jax.ShapeDtypeStruct((256, 256), F32)],
        grid_spec=pltpu.PrefetchScalarGridSpec(
            num_scalar_prefetch=1,
            grid=(4 * chunk,),
            in_specs=[full, full, *specs, wide],
            out_specs=[wide, full],
            scratch_shapes=[pltpu.VMEM((256, 256), BF16), pltpu.VMEM((256, 256), BF16)],
        ),
        compiler_params=pltpu.CompilerParams(vmem_limit_bytes=40 << 20),
    )(place, cross, inverse, *pieces, trailing)


def local(panel_cols, trailing):
    rows_total = trailing.shape[0] * lax.axis_size("rows")
    shrink = 1.0 / math.sqrt(rows_total)
    core = lax.axis_index("rows") % 2
    column = lax.axis_index("cols")
    half = panel_cols.shape[0] // 2
    top, bottom = panel_cols[:half], panel_cols[half:]
    la = lax.ppermute(top, "cols", around(1))
    rb = lax.ppermute(bottom, "cols", around(-1))
    lb = lax.ppermute(bottom, "cols", around(1))
    ra = lax.ppermute(top, "cols", around(-1))
    oa = lax.ppermute(la, "cols", around(1))
    ob = lax.ppermute(rb, "cols", around(-1))

    gram = inner(panel_cols, panel_cols, HIGHEST)
    gram = halves(gram, core)
    gram = exchange_sum(gram, "rows", FIRST)
    gram = exchange_sum(gram, "rows", SECOND)
    gram = exchange_sum(gram, "cols", [around(k) for k in (2, 1, 3)])
    gram = joined(gram, core)
    lower = jnp.linalg.cholesky(gram)
    inverse = jax.scipy.linalg.solve_triangular(lower, jnp.eye(256, dtype=F32), lower=True)

    def rows_of(offset, low, count):
        return lax.dynamic_slice_in_dim(trailing, (column + offset) % 4 * 2 * half + low, count)

    cross = inner(panel_cols, rows_of(0, 0, 2 * half), lax.Precision.HIGH)
    for piece, offset, low in ((la, 3, 0), (rb, 1, half), (lb, 3, half), (ra, 1, 0), (oa, 2, 0), (ob, 2, half)):
        cross = cross + inner(piece, rows_of(offset, low, half), lax.Precision.HIGH)
    cross = halves(cross, core)
    cross = exchange_sum(cross, "rows", FIRST)
    cross = exchange_sum(cross, "rows", SECOND)
    cross = joined(cross, core)

    place = jnp.full((1,), column, jnp.int32)
    updated, r_cross = update(cross, inverse, (panel_cols, la, lb, ra, rb, oa, ob), trailing, place, shrink)
    return (lower.T * shrink, r_cross, updated)


def solution(mesh):
    in_specs = (P(("rows", "cols"), None), P("rows", "cols"))
    out_specs = (P(), P(None, "cols"), P("rows", "cols"))
    return jax.shard_map(local, mesh=mesh, in_specs=in_specs, out_specs=out_specs, check_vma=False)
```

```python
import math

import jax
import jax.numpy as jnp
from jax import lax
from jax.experimental import pallas as pl
from jax.experimental.pallas import tpu as pltpu
from jax.sharding import PartitionSpec as P

F32, BF16 = jnp.float32, jnp.bfloat16
HIGHEST = lax.Precision.HIGHEST
CBLOCK = 1024
UBLOCK = 1024

def split(value):
    high = value.astype(BF16)
    return high, (value - high.astype(F32)).astype(BF16)

def contract(left, right, dims, precision=None):
    return lax.dot_general(left, right, (dims, ((), ())), precision=precision, preferred_element_type=F32)

def factor_block(block, group):
    size = block.shape[0]
    lane = lax.broadcasted_iota(jnp.int32, (size, 2 * size), 1)
    row = lax.broadcasted_iota(jnp.int32, (size, 2 * size), 0)
    wide = jnp.concatenate([block, jnp.zeros((size, size), F32)], axis=1)
    wide = jnp.where(lane == row + size, 1.0, wide)
    for first in range(0, size, group):
        columns = [jnp.broadcast_to(wide[:, first + g : first + g + 1], wide.shape) for g in range(group)]
        rows = [wide[first + g : first + g + 1, :] for g in range(group)]
        small = [[columns[j][first + i : first + i + 1, :] for j in range(group)] for i in range(group)]
        change = None
        for g in range(group):
            inv = 1.0 / small[g][g]
            scaled = rows[g] * inv
            for i in range(g + 1, group):
                ratio = small[i][g] * inv
                rows[i] = rows[i] - ratio * rows[g]
                for j in range(g + 1, group):
                    small[i][j] = small[i][j] - ratio * small[g][j]
            for j in range(g + 1, group):
                columns[j] = columns[j] - columns[g] * (small[g][j] * inv)
            term = jnp.where(row > first + g, columns[g] * scaled, 0.0)
            change = term if change is None else change + term
        wide = wide - change
    diagonal = jnp.sum(jnp.where(lane == row, wide, 0.0), axis=1, keepdims=True)
    wide = wide * lax.rsqrt(diagonal)
    return wide

def factor_kernel(shrink, size, group, core, mine, other, r_factor, inverse, work):
    @pl.when(core[0] == 0)
    def _():
        work[:128, :256] = mine[...]
        work[128:, :256] = other[...]
    @pl.when(core[0] != 0)
    def _():
        work[:128, :256] = other[...]
        work[128:, :256] = mine[...]
    rows = lax.broadcasted_iota(jnp.int32, (256, 256), 0)
    lanes = lax.broadcasted_iota(jnp.int32, (256, 256), 1)
    work[:, 256:] = (rows == lanes).astype(F32)
    for first in range(0, 256, size):
        last = first + size
        both = factor_block(work[first:last, first:last], group)
        done = contract(both[:, size:], work[first:last, :], ((1,), (0,)), HIGHEST)
        work[first:last, :] = done
        if last < 256:
            work[last:, :] -= contract(done[:, last:256], done, ((0,), (0,)), HIGHEST)
    r_factor[...] = jnp.where(rows <= lanes, work[:, :256], 0.0) * shrink
    inverse[...] = jnp.where(rows >= lanes, work[:, 256:], 0.0)

def factor(core, mine, other, shrink, size=64, group=4):
    full = jax.ShapeDtypeStruct((256, 256), F32)
    return pl.pallas_call(
        lambda *refs: factor_kernel(shrink, size, group, *refs),
        out_shape=[full, full],
        in_specs=[pl.BlockSpec(memory_space=pltpu.SMEM), pl.BlockSpec(memory_space=pltpu.VMEM), pl.BlockSpec(memory_space=pltpu.VMEM)],
        out_specs=[pl.BlockSpec(memory_space=pltpu.VMEM)] * 2,
        scratch_shapes=[pltpu.VMEM((256, 512), F32)],
        compiler_params=pltpu.CompilerParams(vmem_limit_bytes=16 << 20),
    )(core, mine, other)

def product3(piece, w):
    high, low = split(piece)
    return contract(jnp.concatenate([high, low, high], axis=1), w[...], ((1,), (0,)))

def update_kernel(shrink, block, piece_rows, place, mine, other, inverse, *refs):
    *pieces, trailing, updated, r_cross, w = refs
    step = pl.program_id(0)

    @pl.when(step == 0)
    def _():
        first = place[1] == 0
        top = jnp.where(first, mine[...], other[...])
        bottom = jnp.where(first, other[...], mine[...])
        cross = jnp.concatenate([top, bottom], axis=0)
        coupling = contract(inverse[...], cross, ((1,), (0,)), HIGHEST)
        r_cross[...] = coupling * shrink
        weights = contract(inverse[...], coupling, ((0,), (0,)), HIGHEST)
        high, low = split(weights)
        w[:256, :] = high
        w[256:512, :] = high
        w[512:, :] = low

    at = at_piece = 0
    for piece in pieces:
        count = piece_rows[at_piece] // block
        at_piece += 1
        @pl.when((step >= at) & (step < at + count))
        def _(piece=piece):
            updated[...] = trailing[...] - product3(piece[...], w)
        at += count

def update(mine, other, inverse, pieces, rows, trailing, place, shrink, block):
    full = pl.BlockSpec((256, 256), lambda i, place: (0, 0))
    half = pl.BlockSpec((128, 256), lambda i, place: (0, 0))
    specs, at = [], 0
    for count in rows:
        count //= block
        specs.append(pl.BlockSpec((block, 256), lambda i, place, at=at, count=count: (jnp.clip(i - at, 0, count - 1), 0)))
        at += count
    chunk = 2048 // block

    def row(i, place):
        which = i // chunk
        offset = jnp.where(which == 0, 0, jnp.where(which == 1, 3, jnp.where(which == 2, 1, 2)))
        return ((place[0] + offset) % 4 * chunk + i % chunk, 0)

    wide = pl.BlockSpec((block, 256), row)
    return pl.pallas_call(
        lambda *refs: update_kernel(shrink, block, rows, *refs),
        out_shape=[jax.ShapeDtypeStruct(trailing.shape, F32), jax.ShapeDtypeStruct((256, 256), F32)],
        grid_spec=pltpu.PrefetchScalarGridSpec(
            num_scalar_prefetch=1, grid=(4 * chunk,),
            in_specs=[half, half, full, *specs, wide], out_specs=[wide, full],
            scratch_shapes=[pltpu.VMEM((768, 256), BF16)]),
        compiler_params=pltpu.CompilerParams(vmem_limit_bytes=48 << 20),
    )(place, mine, other, inverse, *pieces, trailing)

def cross_kernel(counts, initial, halves, place, *refs):
    refs = list(refs)
    start = refs.pop(0) if initial else None
    pieces, refs = refs[:len(counts)], refs[len(counts):]
    trailing, *outs, acc = refs
    step = pl.program_id(0)
    @pl.when(step == 0)
    def _():
        acc[...] = start[...] if initial else jnp.zeros_like(acc)
    at = 0
    for piece, count in zip(pieces, counts):
        @pl.when((step >= at) & (step < at + count))
        def _(piece=piece):
            ph, pb = split(piece[...])
            th, tb = split(trailing[...])
            left = jnp.concatenate([ph, pb, ph], axis=0)
            right = jnp.concatenate([th, th, tb], axis=0)
            acc[...] += contract(left, right, ((0,), (0,)))

        at += count
    @pl.when(step == at - 1)
    def _():
        if halves:
            keep, send = outs
            @pl.when(place[1] == 0)
            def _():
                keep[...] = acc[:128, :]
                send[...] = acc[128:, :]
            @pl.when(place[1] != 0)
            def _():
                keep[...] = acc[128:, :]
                send[...] = acc[:128, :]
        else:
            outs[0][...] = acc[...]

def cross_part(place, initial, pieces, spots, trailing, halves, block, rows):
    counts = [r // block for r in rows]
    full = pl.BlockSpec((256, 256), lambda i, place: (0, 0))
    half = pl.BlockSpec((128, 256), lambda i, place: (0, 0))
    specs, at, table = [], 0, []
    for piece, count, (offset, low) in zip(pieces, counts, spots):
        specs.append(pl.BlockSpec((block, 256), lambda i, place, at=at, count=count: (jnp.clip(i - at, 0, count - 1), 0)))
        table += [(offset, low // block + n) for n in range(count)]
        at += count
    def row(i, place):
        offset, low = table[-1]
        off, lo = jnp.int32(offset), jnp.int32(low)
        for n in range(at - 1):
            off = jnp.where(i == n, table[n][0], off)
            lo = jnp.where(i == n, table[n][1], lo)
        return ((place[0] + off) % 4 * (2048 // block) + lo, 0)
    out = [jax.ShapeDtypeStruct((128, 256), F32)] * 2 if halves else [jax.ShapeDtypeStruct((256, 256), F32)]
    return pl.pallas_call(
        lambda *refs: cross_kernel(counts, initial is not None, halves, *refs),
        out_shape=out,
        grid_spec=pltpu.PrefetchScalarGridSpec(
            num_scalar_prefetch=1, grid=(at,),
            in_specs=([full] if initial is not None else []) + specs + [pl.BlockSpec((block, 256), row)],
            out_specs=[half, half] if halves else [full],
            scratch_shapes=[pltpu.VMEM((256, 256), F32)]),
        compiler_params=pltpu.CompilerParams(vmem_limit_bytes=48 << 20),
    )(place, *([initial] if initial is not None else []), *pieces, trailing)


def gram_kernel(place, panel, keep, send):
    @pl.when(pl.program_id(0) == 0)
    def _():
        keep[...] = jnp.zeros_like(keep)
        send[...] = jnp.zeros_like(send)
    part = contract(panel[...], panel[...], ((0,), (0,)), HIGHEST)
    @pl.when(place[1] == 0)
    def _():
        keep[...] += part[:128, :]
        send[...] += part[128:, :]
    @pl.when(place[1] != 0)
    def _():
        keep[...] += part[128:, :]
        send[...] += part[:128, :]

def gram_part(place, panel, block=1024):
    half = pl.BlockSpec((128, 256), lambda i, place: (0, 0))
    return pl.pallas_call(
        gram_kernel,
        out_shape=[jax.ShapeDtypeStruct((128, 256), F32)] * 2,
        grid_spec=pltpu.PrefetchScalarGridSpec(
            num_scalar_prefetch=1, grid=(panel.shape[0] // block,),
            in_specs=[pl.BlockSpec((block, 256), lambda i, place: (i, 0))],
            out_specs=[half, half]),
        compiler_params=pltpu.CompilerParams(vmem_limit_bytes=32 << 20),
    )(place, panel)


def over_rows(move):
    pairs = []
    for z in range(4):
        for x in range(4):
            for core in range(2):
                z2, x2, core2 = move(z, x, core)
                pairs.append(((z * 4 + x) * 2 + core, (z2 % 4 * 4 + x2 % 4) * 2 + core2))
    return pairs


PARTNER = over_rows(lambda z, x, core: (z, x, 1 - core))
FIRST = [over_rows(lambda z, x, core, k=k: (z, x + k, core) if core == 0 else (z + k, x, core)) for k in (2, 1, 3)]
SECOND = [over_rows(lambda z, x, core, k=k: (z + k, x, core) if core == 0 else (z, x + k, core)) for k in (2, 1, 3)]


def around(k):
    return [(i, (i + k) % 4) for i in range(4)]


def exchange_sum(part, axis, moves):
    others = [lax.ppermute(part, axis, move) for move in moves]
    return part + others[0] + others[1] + others[2]


def partner(part):
    return lax.ppermute(part, "rows", PARTNER)


def local(panel_cols, trailing):
    rows_total = trailing.shape[0] * lax.axis_size("rows")
    shrink = 1.0 / math.sqrt(rows_total)
    core = lax.axis_index("rows") % 2
    place = jnp.stack([lax.axis_index("cols"), core]).astype(jnp.int32)
    size = panel_cols.shape[0]
    half = size // 2
    barrier = lax.optimization_barrier
    left1 = lax.ppermute(panel_cols[:half], "cols", around(1))
    right1 = lax.ppermute(panel_cols[half:], "cols", around(-1))

    keep, send = gram_part(place, panel_cols)
    gram = keep + partner(send)
    left1, right1, _, rest = barrier((left1, right1, gram, panel_cols))
    gram = exchange_sum(gram, "cols", [around(k) for k in (2, 1, 3)])
    left2 = lax.ppermute(rest[half:], "cols", around(1))
    right2 = lax.ppermute(rest[:half], "cols", around(-1))
    far1 = lax.ppermute(left1, "cols", around(1))
    far2 = lax.ppermute(right1, "cols", around(-1))
    gram = exchange_sum(gram, "rows", FIRST)
    gram = exchange_sum(gram, "rows", SECOND)
    r_factor, inverse = factor(place[1:], gram, partner(gram), shrink, 64, 8)

    rows = (size, half, half)
    (cross,) = cross_part(place, None, (panel_cols, left1, right1), ((0, 0), (3, 0), (1, half)), trailing, False, CBLOCK, rows=rows)
    (cross,) = cross_part(place, cross, (left2, right2), ((3, half), (1, 0)), trailing, False, CBLOCK, rows=(half, half))
    inverse, far1, far2 = barrier((inverse, far1, far2))
    keep, send = cross_part(place, cross, (far1, far2), ((2, 0), (2, half)), trailing, True, CBLOCK, rows=(half, half))
    cross = keep + partner(send)
    cross = exchange_sum(cross, "rows", FIRST)
    cross = exchange_sum(cross, "rows", SECOND)
    pieces = (panel_cols, left1, left2, right2, right1, far1, far2)
    rows = (size, half, half, half, half, half, half)
    updated, r_cross = update(cross, partner(cross), inverse, pieces, rows, trailing, place, shrink, UBLOCK)
    return (r_factor, r_cross, updated)


def solution(mesh):
    in_specs = (P(("rows", "cols"), None), P("rows", "cols"))
    out_specs = (P(), P(None, "cols"), P("rows", "cols"))
    return jax.shard_map(local, mesh=mesh, in_specs=in_specs, out_specs=out_specs, check_vma=False)
```

```python
import math

import jax
import jax.numpy as jnp
from jax import lax
from jax.experimental import pallas as pl
from jax.experimental.pallas import tpu as pltpu
from jax.sharding import PartitionSpec as P

F32, BF16 = jnp.float32, jnp.bfloat16
HIGHEST = lax.Precision.HIGHEST
BLOCK = 512
UPDATE_VMEM = 28 << 20
CROSS_VMEM = 16 << 20

def split(value):
    high = value.astype(BF16)
    return high, (value - high.astype(F32)).astype(BF16)

def contract(left, right, dims, precision=None):
    return lax.dot_general(left, right, (dims, ((), ())), precision=precision, preferred_element_type=F32)

def factor_block(block, group):
    size = block.shape[0]
    lane = lax.broadcasted_iota(jnp.int32, (size, 2 * size), 1)
    row = lax.broadcasted_iota(jnp.int32, (size, 2 * size), 0)
    wide = jnp.concatenate([block, jnp.zeros((size, size), F32)], axis=1)
    wide = jnp.where(lane == row + size, 1.0, wide)
    for first in range(0, size, group):
        columns = [jnp.broadcast_to(wide[:, first + g : first + g + 1], wide.shape) for g in range(group)]
        rows = [wide[first + g : first + g + 1, :] for g in range(group)]
        small = [[columns[j][first + i : first + i + 1, :] for j in range(group)] for i in range(group)]
        change = None
        for g in range(group):
            inv = 1.0 / small[g][g]
            scaled = rows[g] * inv
            for i in range(g + 1, group):
                ratio = small[i][g] * inv
                rows[i] = rows[i] - ratio * rows[g]
                for j in range(g + 1, group):
                    small[i][j] = small[i][j] - ratio * small[g][j]
            for j in range(g + 1, group):
                columns[j] = columns[j] - columns[g] * (small[g][j] * inv)
            term = jnp.where(row > first + g, columns[g] * scaled, 0.0)
            change = term if change is None else change + term
        wide = wide - change
    diagonal = jnp.sum(jnp.where(lane == row, wide, 0.0), axis=1, keepdims=True)
    wide = wide * lax.rsqrt(diagonal)
    return wide

def factor_kernel(shrink, size, group, core, mine, other, r_factor, inverse, work):
    @pl.when(core[0] == 0)
    def _():
        work[:128, :256] = mine[...]
        work[128:, :256] = other[...]
    @pl.when(core[0] != 0)
    def _():
        work[:128, :256] = other[...]
        work[128:, :256] = mine[...]
    rows = lax.broadcasted_iota(jnp.int32, (256, 256), 0)
    lanes = lax.broadcasted_iota(jnp.int32, (256, 256), 1)
    work[:, 256:] = (rows == lanes).astype(F32)
    for first in range(0, 256, size):
        last = first + size
        both = factor_block(work[first:last, first:last], group)
        done = contract(both[:, size:], work[first:last, :], ((1,), (0,)), HIGHEST)
        work[first:last, :] = done
        if last < 256:
            work[last:, :] -= contract(done[:, last:256], done, ((0,), (0,)), HIGHEST)
    r_factor[...] = jnp.where(rows <= lanes, work[:, :256], 0.0) * shrink
    inverse[...] = jnp.where(rows >= lanes, work[:, 256:], 0.0)

def factor(core, mine, other, shrink, size=64, group=4):
    full = jax.ShapeDtypeStruct((256, 256), F32)
    return pl.pallas_call(
        lambda *refs: factor_kernel(shrink, size, group, *refs),
        out_shape=[full, full],
        in_specs=[pl.BlockSpec(memory_space=pltpu.SMEM), pl.BlockSpec(memory_space=pltpu.VMEM), pl.BlockSpec(memory_space=pltpu.VMEM)],
        out_specs=[pl.BlockSpec(memory_space=pltpu.VMEM)] * 2,
        scratch_shapes=[pltpu.VMEM((256, 512), F32)],
        cost_estimate=pl.CostEstimate(flops=8000000000, bytes_accessed=0, transcendentals=0),
        compiler_params=pltpu.CompilerParams(vmem_limit_bytes=16 << 20),
    )(core, mine, other)

def blocks_of(pieces, block):
    return [
        (n, row, offset, low + row)
        for n, (count, offset, low) in enumerate(pieces)
        for row in range(0, count, block)
    ]


def rows_at(column, offset, low, chunk, block):
    return pl.ds(pl.multiple_of(lax.rem(column + offset, 4) * chunk + low, block), block)


def update_kernel(shrink, blocks, block, chunk, place, mine, other, inverse, *refs):
    *pieces, trailing, updated, r_cross, result, weights, sems = refs
    first = place[1] == 0
    top = jnp.where(first, mine[...], other[...])
    bottom = jnp.where(first, other[...], mine[...])
    coupling = contract(inverse[...], jnp.concatenate([top, bottom], axis=0), ((1,), (0,)), HIGHEST)
    r_cross[...] = coupling * shrink
    high, low = split(contract(inverse[...], coupling, ((0,), (0,)), HIGHEST))
    weights[:256, :] = high
    weights[256:512, :] = high
    weights[512:, :] = low
    stores = []
    for n, (piece, row, offset, low_row) in enumerate(blocks):
        rows = rows_at(place[0], offset, low_row, chunk, block)
        high, low = split(pieces[piece][row : row + block, :])
        product = contract(jnp.concatenate([high, low, high], axis=1), weights[...], ((1,), (0,)))
        here = pl.ds(n * block, block)
        result[here, :] = trailing[rows, :] - product
        store = pltpu.make_async_copy(result.at[here], updated.at[rows], sems.at[n])
        store.start()
        stores.append(store)
    for store in stores:
        store.wait()


def update(mine, other, inverse, pieces, spots, trailing, place, shrink, block):
    blocks = blocks_of(spots, block)
    vmem, anywhere = pl.BlockSpec(memory_space=pltpu.VMEM), pl.BlockSpec(memory_space=pl.ANY)
    total = trailing.shape[0]
    return pl.pallas_call(
        lambda *refs: update_kernel(shrink, blocks, block, total // 4, *refs),
        out_shape=[jax.ShapeDtypeStruct(trailing.shape, F32), jax.ShapeDtypeStruct((256, 256), F32)],
        in_specs=[pl.BlockSpec(memory_space=pltpu.SMEM), *[vmem] * (len(pieces) + 4)],
        out_specs=[anywhere, vmem],
        scratch_shapes=[
            pltpu.VMEM((total, 256), F32),
            pltpu.VMEM((768, 256), BF16),
            pltpu.SemaphoreType.DMA((len(blocks),)),
        ],
        compiler_params=pltpu.CompilerParams(vmem_limit_bytes=UPDATE_VMEM),
    )(place, mine, other, inverse, *pieces, trailing)


def cross_kernel(initial, halves, blocks, block, chunk, place, *refs):
    refs = list(refs)
    total = refs.pop(0)[...] if initial else None
    count = 2 if halves else 1
    *pieces, trailing = refs[:-count]
    outs = refs[-count:]
    for piece, row, offset, low in blocks:
        left = split(pieces[piece][row : row + block, :])
        right = split(trailing[rows_at(place[0], offset, low, chunk, block), :])
        product = contract(
            jnp.concatenate([left[0], left[1], left[0]], axis=0),
            jnp.concatenate([right[0], right[0], right[1]], axis=0),
            ((0,), (0,)),
        )
        total = product if total is None else total + product
    if halves:
        first = place[1] == 0
        outs[0][...] = jnp.where(first, total[:128, :], total[128:, :])
        outs[1][...] = jnp.where(first, total[128:, :], total[:128, :])
    else:
        outs[0][...] = total


def cross_part(place, initial, pieces, spots, trailing, halves, block):
    blocks = blocks_of(spots, block)
    vmem = pl.BlockSpec(memory_space=pltpu.VMEM)
    given = [] if initial is None else [initial]
    shapes = [(128, 256)] * 2 if halves else [(256, 256)]
    return pl.pallas_call(
        lambda *refs: cross_kernel(bool(given), halves, blocks, block, trailing.shape[0] // 4, *refs),
        out_shape=[jax.ShapeDtypeStruct(shape, F32) for shape in shapes],
        in_specs=[pl.BlockSpec(memory_space=pltpu.SMEM), *[vmem] * (len(given) + len(pieces) + 1)],
        out_specs=[vmem] * len(shapes),
        compiler_params=pltpu.CompilerParams(vmem_limit_bytes=CROSS_VMEM),
    )(place, *given, *pieces, trailing)


def gram_kernel(place, panel, keep, send):
    @pl.when(pl.program_id(0) == 0)
    def _():
        keep[...] = jnp.zeros_like(keep)
        send[...] = jnp.zeros_like(send)
    part = contract(panel[...], panel[...], ((0,), (0,)), HIGHEST)
    @pl.when(place[1] == 0)
    def _():
        keep[...] += part[:128, :]
        send[...] += part[128:, :]
    @pl.when(place[1] != 0)
    def _():
        keep[...] += part[128:, :]
        send[...] += part[:128, :]

def gram_part(place, panel, block=1024):
    half = pl.BlockSpec((128, 256), lambda i, place: (0, 0))
    return pl.pallas_call(
        gram_kernel,
        out_shape=[jax.ShapeDtypeStruct((128, 256), F32)] * 2,
        grid_spec=pltpu.PrefetchScalarGridSpec(
            num_scalar_prefetch=1, grid=(panel.shape[0] // block,),
            in_specs=[pl.BlockSpec((block, 256), lambda i, place: (i, 0))],
            out_specs=[half, half]),
        compiler_params=pltpu.CompilerParams(vmem_limit_bytes=32 << 20),
    )(place, panel)


def over_rows(move):
    pairs = []
    for z in range(4):
        for x in range(4):
            for core in range(2):
                z2, x2, core2 = move(z, x, core)
                pairs.append(((z * 4 + x) * 2 + core, (z2 % 4 * 4 + x2 % 4) * 2 + core2))
    return pairs


ORDER = (1, 3, 2)


PARTNER = over_rows(lambda z, x, core: (z, x, 1 - core))
FIRST = [over_rows(lambda z, x, core, k=k: (z, x + k, core) if core == 0 else (z + k, x, core)) for k in ORDER]
SECOND = [over_rows(lambda z, x, core, k=k: (z + k, x, core) if core == 0 else (z, x + k, core)) for k in ORDER]


def around(k):
    return [(i, (i + k) % 4) for i in range(4)]


def move(name, part, axis, pairs):
    with jax.named_scope(name):
        return lax.ppermute(part, axis, pairs)


def exchange_sum(name, part, axis, moves):
    others = [move(name, part, axis, pairs) for pairs in moves]
    return (part + others[2]) + (others[0] + others[1])


def partner(name, part):
    return move(name, part, "rows", PARTNER)


def local(panel_cols, trailing):
    rows_total = trailing.shape[0] * lax.axis_size("rows")
    shrink = 1.0 / math.sqrt(rows_total)
    core = lax.axis_index("rows") % 2
    place = jnp.stack([lax.axis_index("cols"), core]).astype(jnp.int32)
    size = panel_cols.shape[0]
    half = size // 2
    barrier = lax.optimization_barrier
    left = move("left", panel_cols, "cols", around(1))
    right = move("right", panel_cols, "cols", around(-1))

    keep, send = gram_part(place, panel_cols)
    gram = keep + partner("gram_halves", send)
    gram = exchange_sum("gram_first", gram, "rows", FIRST)
    gram = exchange_sum("gram_second", gram, "rows", SECOND)
    left, _ = barrier((left, gram))
    right, _ = barrier((right, gram))
    far1 = move("far1", left[:half], "cols", around(1))
    far2 = move("far2", right[half:], "cols", around(-1))
    gram = exchange_sum("gram_cols", gram, "cols", [around(k) for k in ORDER])
    r_factor, inverse = factor(place[1:], gram, partner("gram_join", gram), shrink, 64, 8)

    (cross,) = cross_part(place, None, (panel_cols, left, right), ((size, 0, 0), (size, 3, 0), (size, 1, 0)), trailing, False, BLOCK)
    inverse, far1, far2, cross = barrier((inverse, far1, far2, cross))
    keep, send = cross_part(place, cross, (far1, far2), ((half, 2, 0), (half, 2, half)), trailing, True, BLOCK)
    cross = keep + partner("cross_halves", send)
    cross = exchange_sum("cross_first", cross, "rows", FIRST)
    cross = exchange_sum("cross_second", cross, "rows", SECOND)
    pieces = (panel_cols, left, right, far1, far2)
    spots = ((size, 0, 0), (size, 3, 0), (size, 1, 0), (half, 2, 0), (half, 2, half))
    updated, r_cross = update(cross, partner("cross_join", cross), inverse, pieces, spots, trailing, place, shrink, BLOCK)
    return (r_factor, r_cross, updated)


def solution(mesh):
    in_specs = (P(("rows", "cols"), None), P("rows", "cols"))
    out_specs = (P(), P(None, "cols"), P("rows", "cols"))
    return jax.shard_map(local, mesh=mesh, in_specs=in_specs, out_specs=out_specs, check_vma=False)
```

```python
import math

import jax
import jax.numpy as jnp
from jax import lax
from jax.experimental import pallas as pl
from jax.experimental.pallas import tpu as pltpu
from jax.sharding import PartitionSpec as P

F32, BF16 = jnp.float32, jnp.bfloat16
HIGHEST = lax.Precision.HIGHEST
BLOCK = 512
UPDATE_VMEM = 14 << 20
CROSS_VMEM = 8 << 20

def split(value):
    high = value.astype(BF16)
    return high, (value - high.astype(F32)).astype(BF16)

def contract(left, right, dims, precision=None):
    return lax.dot_general(left, right, (dims, ((), ())), precision=precision, preferred_element_type=F32)

def factor_block(block, group):
    size = block.shape[0]
    lane = lax.broadcasted_iota(jnp.int32, (size, 2 * size), 1)
    row = lax.broadcasted_iota(jnp.int32, (size, 2 * size), 0)
    wide = jnp.concatenate([block, jnp.zeros((size, size), F32)], axis=1)
    wide = jnp.where(lane == row + size, 1.0, wide)
    for first in range(0, size, group):
        columns = [jnp.broadcast_to(wide[:, first + g : first + g + 1], wide.shape) for g in range(group)]
        rows = [wide[first + g : first + g + 1, :] for g in range(group)]
        small = [[columns[j][first + i : first + i + 1, :] for j in range(group)] for i in range(group)]
        change = None
        for g in range(group):
            inv = 1.0 / small[g][g]
            scaled = rows[g] * inv
            for i in range(g + 1, group):
                ratio = small[i][g] * inv
                rows[i] = rows[i] - ratio * rows[g]
                for j in range(g + 1, group):
                    small[i][j] = small[i][j] - ratio * small[g][j]
            for j in range(g + 1, group):
                columns[j] = columns[j] - columns[g] * (small[g][j] * inv)
            term = jnp.where(row > first + g, columns[g] * scaled, 0.0)
            change = term if change is None else change + term
        wide = wide - change
    diagonal = jnp.sum(jnp.where(lane == row, wide, 0.0), axis=1, keepdims=True)
    wide = wide * lax.rsqrt(diagonal)
    return wide

def factor_kernel(shrink, size, group, mine, other, r_factor, inverse, work):
    _, first = whereabouts()
    one = jnp.where(first, mine[...], other[...])
    two = jnp.where(first, other[...], mine[...])
    work[:128, :128] = one[:128, :]
    work[:64, 128:256] = one[128:, :]
    work[64:128, 128:256] = two[128:, :]
    work[128:, :128] = jnp.zeros((128, 128), F32)
    work[128:, 128:256] = two[:128, :]
    rows = lax.broadcasted_iota(jnp.int32, (256, 256), 0)
    lanes = lax.broadcasted_iota(jnp.int32, (256, 256), 1)
    work[:, 256:] = (rows == lanes).astype(F32)
    for first in range(0, 256, size):
        last = first + size
        both = factor_block(work[first:last, first:last], group)
        done = contract(both[:, size:], work[first:last, :], ((1,), (0,)), HIGHEST)
        work[first:last, :] = done
        if last < 256:
            work[last:, :] -= contract(done[:, last:256], done, ((0,), (0,)), HIGHEST)
    r_factor[...] = jnp.where(rows <= lanes, work[:, :256], 0.0) * shrink
    inverse[...] = jnp.where(rows >= lanes, work[:, 256:], 0.0)

def factor(mine, other, shrink, size=64, group=4):
    full = jax.ShapeDtypeStruct((256, 256), F32)
    return pl.pallas_call(
        lambda *refs: factor_kernel(shrink, size, group, *refs),
        out_shape=[full, full],
        in_specs=[pl.BlockSpec(memory_space=pltpu.VMEM)] * 2,
        out_specs=[pl.BlockSpec(memory_space=pltpu.VMEM)] * 2,
        scratch_shapes=[pltpu.VMEM((256, 512), F32)],
        cost_estimate=pl.CostEstimate(flops=8000000000, bytes_accessed=0, transcendentals=0),
        compiler_params=pltpu.CompilerParams(vmem_limit_bytes=16 << 20),
    )(mine, other)

def whereabouts():
    return lax.axis_index("cols"), lax.rem(lax.axis_index("rows"), 2) == 0


def blocks_of(pieces, block):
    return [
        (n, row, offset, low + row)
        for n, (count, offset, low) in enumerate(pieces)
        for row in range(0, count, block)
    ]


def rows_at(column, offset, low, chunk, block):
    return pl.ds(pl.multiple_of(lax.rem(column + offset, 4) * chunk + low, block), block)


def update_kernel(shrink, blocks, block, chunk, mine, other, inverse, *refs):
    *pieces, trailing, updated, r_cross, result, weights, sems = refs
    column, first = whereabouts()
    top = jnp.where(first, mine[...], other[...])
    bottom = jnp.where(first, other[...], mine[...])
    coupling = contract(inverse[...], jnp.concatenate([top, bottom], axis=0), ((1,), (0,)), HIGHEST)
    r_cross[...] = coupling * shrink
    high, low = split(contract(inverse[...], coupling, ((0,), (0,)), HIGHEST))
    weights[:256, :] = high
    weights[256:512, :] = high
    weights[512:, :] = low
    stores = []
    for n, (piece, row, offset, low_row) in enumerate(blocks):
        rows = rows_at(column, offset, low_row, chunk, block)
        high, low = split(pieces[piece][row : row + block, :])
        product = contract(jnp.concatenate([high, low, high], axis=1), weights[...], ((1,), (0,)))
        here = pl.ds(n * block, block)
        result[here, :] = trailing[rows, :] - product
        store = pltpu.make_async_copy(result.at[here], updated.at[rows], sems.at[n])
        store.start()
        stores.append(store)
    for store in stores:
        store.wait()


def update(mine, other, inverse, pieces, spots, trailing, shrink, block):
    blocks = blocks_of(spots, block)
    vmem, anywhere = pl.BlockSpec(memory_space=pltpu.VMEM), pl.BlockSpec(memory_space=pl.ANY)
    total = trailing.shape[0]
    return pl.pallas_call(
        lambda *refs: update_kernel(shrink, blocks, block, total // 4, *refs),
        out_shape=[jax.ShapeDtypeStruct(trailing.shape, F32), jax.ShapeDtypeStruct((256, 256), F32)],
        in_specs=[vmem] * (len(pieces) + 4),
        out_specs=[anywhere, vmem],
        scratch_shapes=[
            pltpu.VMEM((total, 256), F32),
            pltpu.VMEM((768, 256), BF16),
            pltpu.SemaphoreType.DMA((len(blocks),)),
        ],
        compiler_params=pltpu.CompilerParams(vmem_limit_bytes=UPDATE_VMEM),
    )(mine, other, inverse, *pieces, trailing)


def cross_kernel(initial, halves, blocks, block, chunk, *refs):
    refs = list(refs)
    column, first = whereabouts()
    total = refs.pop(0)[...] if initial else None
    count = 2 if halves else 1
    *pieces, trailing = refs[:-count]
    outs = refs[-count:]
    for piece, row, offset, low in blocks:
        left = split(pieces[piece][row : row + block, :])
        right = split(trailing[rows_at(column, offset, low, chunk, block), :])
        product = contract(
            jnp.concatenate([left[0], left[1], left[0]], axis=0),
            jnp.concatenate([right[0], right[0], right[1]], axis=0),
            ((0,), (0,)),
        )
        total = product if total is None else total + product
    if halves:
        outs[0][...] = jnp.where(first, total[:128, :], total[128:, :])
        outs[1][...] = jnp.where(first, total[128:, :], total[:128, :])
    else:
        outs[0][...] = total


def cross_part(initial, pieces, spots, trailing, halves, block):
    blocks = blocks_of(spots, block)
    vmem = pl.BlockSpec(memory_space=pltpu.VMEM)
    given = [] if initial is None else [initial]
    shapes = [(128, 256)] * 2 if halves else [(256, 256)]
    return pl.pallas_call(
        lambda *refs: cross_kernel(bool(given), halves, blocks, block, trailing.shape[0] // 4, *refs),
        out_shape=[jax.ShapeDtypeStruct(shape, F32) for shape in shapes],
        in_specs=[vmem] * (len(given) + len(pieces) + 1),
        out_specs=[vmem] * len(shapes),
        compiler_params=pltpu.CompilerParams(vmem_limit_bytes=CROSS_VMEM),
    )(*given, *pieces, trailing)


def gram_kernel(panel, keep, send):
    gram = contract(panel[...], panel[...], ((0,), (0,)), HIGHEST)
    one = jnp.concatenate([gram[:128, :128], gram[:64, 128:]], axis=0)
    two = jnp.concatenate([gram[128:, 128:], gram[64:128, 128:]], axis=0)
    _, first = whereabouts()
    keep[...] = jnp.where(first, one, two)
    send[...] = jnp.where(first, two, one)


def gram_part(panel):
    vmem = pl.BlockSpec(memory_space=pltpu.VMEM)
    return pl.pallas_call(
        gram_kernel,
        out_shape=[jax.ShapeDtypeStruct((192, 128), F32)] * 2,
        in_specs=[vmem],
        out_specs=[vmem, vmem],
        compiler_params=pltpu.CompilerParams(vmem_limit_bytes=16 << 20),
    )(panel)


def over_rows(move):
    pairs = []
    for z in range(4):
        for x in range(4):
            for core in range(2):
                z2, x2, core2 = move(z, x, core)
                pairs.append(((z * 4 + x) * 2 + core, (z2 % 4 * 4 + x2 % 4) * 2 + core2))
    return pairs


ORDER = (1, 3, 2)


PARTNER = over_rows(lambda z, x, core: (z, x, 1 - core))
FIRST = [over_rows(lambda z, x, core, k=k: (z, x + k, core) if core == 0 else (z + k, x, core)) for k in ORDER]
SECOND = [over_rows(lambda z, x, core, k=k: (z + k, x, core) if core == 0 else (z, x + k, core)) for k in ORDER]


def around(k):
    return [(i, (i + k) % 4) for i in range(4)]


def move(name, part, axis, pairs):
    with jax.named_scope(name):
        return lax.ppermute(part, axis, pairs)


def exchange_sum(name, part, axis, moves):
    others = [move(name, part, axis, pairs) for pairs in moves]
    return (others[0] + others[1]) + (part + others[2])


def partner(name, part):
    return move(name, part, "rows", PARTNER)


def local(panel_cols, trailing):
    rows_total = trailing.shape[0] * lax.axis_size("rows")
    shrink = 1.0 / math.sqrt(rows_total)
    size = panel_cols.shape[0]
    half = size // 2
    barrier = lax.optimization_barrier
    left = move("left", panel_cols, "cols", around(1))
    right = move("right", panel_cols, "cols", around(-1))

    keep, send = gram_part(panel_cols)
    gram = keep + partner("gram_halves", send)
    gram = exchange_sum("gram_first", gram, "rows", FIRST)
    gram = exchange_sum("gram_second", gram, "rows", SECOND)
    left, _ = barrier((left, gram))
    right, _ = barrier((right, gram))
    far1 = move("far1", left[:half], "cols", around(1))
    far2 = move("far2", right[half:], "cols", around(-1))
    gram = exchange_sum("gram_cols", gram, "cols", [around(k) for k in ORDER])
    r_factor, inverse = factor(gram, partner("gram_join", gram), shrink, 64, 8)

    (cross,) = cross_part(None, (panel_cols, left, right), ((size, 0, 0), (size, 3, 0), (size, 1, 0)), trailing, False, BLOCK)
    (cross,) = cross_part(cross, (far2,), ((half, 2, half),), trailing, False, BLOCK)
    inverse, far1, cross = barrier((inverse, far1, cross))
    keep, send = cross_part(cross, (far1,), ((half, 2, 0),), trailing, True, BLOCK)
    cross = keep + partner("cross_halves", send)
    cross = exchange_sum("cross_first", cross, "rows", FIRST)
    cross = exchange_sum("cross_second", cross, "rows", SECOND)
    pieces = (panel_cols, left, right, far1, far2)
    spots = ((size, 0, 0), (size, 3, 0), (size, 1, 0), (half, 2, 0), (half, 2, half))
    updated, r_cross = update(cross, partner("cross_join", cross), inverse, pieces, spots, trailing, shrink, BLOCK)
    return (r_factor, r_cross, updated)


def solution(mesh):
    in_specs = (P(("rows", "cols"), None), P("rows", "cols"))
    out_specs = (P(), P(None, "cols"), P("rows", "cols"))
    return jax.shard_map(local, mesh=mesh, in_specs=in_specs, out_specs=out_specs, check_vma=False)
```

```python
import math

import jax
import jax.numpy as jnp
from jax import lax
from jax.experimental import pallas as pl
from jax.experimental.pallas import tpu as pltpu
from jax.sharding import PartitionSpec as P

F32, BF16 = jnp.float32, jnp.bfloat16
HIGHEST = lax.Precision.HIGHEST
BLOCK = 512
UPDATE_VMEM = 14 << 20
CROSS_VMEM = 8 << 20

def split(value):
    high = value.astype(BF16)
    return high, (value - high.astype(F32)).astype(BF16)

def contract(left, right, dims, precision=None):
    return lax.dot_general(left, right, (dims, ((), ())), precision=precision, preferred_element_type=F32)

def factor_block(block, group):
    size = block.shape[0]
    lane = lax.broadcasted_iota(jnp.int32, (size, 2 * size), 1)
    row = lax.broadcasted_iota(jnp.int32, (size, 2 * size), 0)
    wide = jnp.concatenate([block, jnp.zeros((size, size), F32)], axis=1)
    wide = jnp.where(lane == row + size, 1.0, wide)
    for first in range(0, size, group):
        columns = [jnp.broadcast_to(wide[:, first + g : first + g + 1], wide.shape) for g in range(group)]
        rows = [wide[first + g : first + g + 1, :] for g in range(group)]
        small = [[columns[j][first + i : first + i + 1, :] for j in range(group)] for i in range(group)]
        change = None
        for g in range(group):
            inv = 1.0 / small[g][g]
            scaled = rows[g] * inv
            for i in range(g + 1, group):
                ratio = small[i][g] * inv
                rows[i] = rows[i] - ratio * rows[g]
                for j in range(g + 1, group):
                    small[i][j] = small[i][j] - ratio * small[g][j]
            for j in range(g + 1, group):
                columns[j] = columns[j] - columns[g] * (small[g][j] * inv)
            term = jnp.where(row > first + g, columns[g] * scaled, 0.0)
            change = term if change is None else change + term
        wide = wide - change
    diagonal = jnp.sum(jnp.where(lane == row, wide, 0.0), axis=1, keepdims=True)
    wide = wide * lax.rsqrt(diagonal)
    return wide

def factor_kernel(shrink, size, group, mine, other, r_factor, inverse, gram_inverse, work):
    _, first = whereabouts()
    one = jnp.where(first, mine[...], other[...])
    two = jnp.where(first, other[...], mine[...])
    work[:128, :128] = one[:128, :]
    work[:64, 128:256] = one[128:, :]
    work[64:128, 128:256] = two[128:, :]
    work[128:, :128] = jnp.zeros((128, 128), F32)
    work[128:, 128:256] = two[:128, :]
    rows = lax.broadcasted_iota(jnp.int32, (256, 256), 0)
    lanes = lax.broadcasted_iota(jnp.int32, (256, 256), 1)
    work[:, 256:] = (rows == lanes).astype(F32)
    for first in range(0, 256, size):
        last = first + size
        both = factor_block(work[first:last, first:last], group)
        done = contract(both[:, size:], work[first:last, :], ((1,), (0,)), HIGHEST)
        work[first:last, :] = done
        if last < 256:
            work[last:, :] -= contract(done[:, last:256], done, ((0,), (0,)), HIGHEST)
    r_factor[...] = jnp.where(rows <= lanes, work[:, :256], 0.0) * shrink
    lower = jnp.where(rows >= lanes, work[:, 256:], 0.0)
    inverse[...] = lower
    gram_inverse[...] = contract(lower, lower, ((0,), (0,)), HIGHEST)

def factor(mine, other, shrink, size=64, group=4):
    full = jax.ShapeDtypeStruct((256, 256), F32)
    return pl.pallas_call(
        lambda *refs: factor_kernel(shrink, size, group, *refs),
        out_shape=[full, full, full],
        in_specs=[pl.BlockSpec(memory_space=pltpu.VMEM)] * 2,
        out_specs=[pl.BlockSpec(memory_space=pltpu.VMEM)] * 3,
        scratch_shapes=[pltpu.VMEM((256, 512), F32)],
        cost_estimate=pl.CostEstimate(flops=8000000000, bytes_accessed=0, transcendentals=0),
        compiler_params=pltpu.CompilerParams(vmem_limit_bytes=16 << 20),
    )(mine, other)

def whereabouts():
    return lax.axis_index("cols"), lax.rem(lax.axis_index("rows"), 2) == 0


def blocks_of(pieces, block):
    return [
        (n, row, offset, low + row)
        for n, (count, offset, low) in enumerate(pieces)
        for row in range(0, count, block)
    ]


def rows_at(column, offset, low, chunk, block):
    return pl.ds(pl.multiple_of(lax.rem(column + offset, 4) * chunk + low, block), block)


def update_kernel(shrink, blocks, block, chunk, mine, other, inverse, gram_inverse, *refs):
    *pieces, trailing, updated, r_cross, result, weights, sems = refs
    column, first = whereabouts()
    top = jnp.where(first, mine[...], other[...])
    bottom = jnp.where(first, other[...], mine[...])
    cross = jnp.concatenate([top, bottom], axis=0)
    weights[:256, :], weights[256:, :] = split(contract(gram_inverse[...], cross, ((1,), (0,)), HIGHEST))
    stores = []
    for n, (piece, row, offset, low_row) in enumerate(blocks):
        rows = rows_at(column, offset, low_row, chunk, block)
        high, low = split(pieces[piece][row : row + block, :])
        product = contract(high, weights[:256, :], ((1,), (0,)))
        product += contract(low, weights[:256, :], ((1,), (0,)))
        product += contract(high, weights[256:, :], ((1,), (0,)))
        here = pl.ds(n * block, block)
        result[here, :] = trailing[rows, :] - product
        store = pltpu.make_async_copy(result.at[here], updated.at[rows], sems.at[n])
        store.start()
        stores.append(store)
    r_cross[...] = contract(inverse[...], cross, ((1,), (0,)), HIGHEST) * shrink
    for store in stores:
        store.wait()


def update(mine, other, inverse, gram_inverse, pieces, spots, trailing, shrink, block):
    blocks = blocks_of(spots, block)
    vmem, anywhere = pl.BlockSpec(memory_space=pltpu.VMEM), pl.BlockSpec(memory_space=pl.ANY)
    total = trailing.shape[0]
    return pl.pallas_call(
        lambda *refs: update_kernel(shrink, blocks, block, total // 4, *refs),
        out_shape=[jax.ShapeDtypeStruct(trailing.shape, F32), jax.ShapeDtypeStruct((256, 256), F32)],
        in_specs=[vmem] * (len(pieces) + 5),
        out_specs=[anywhere, vmem],
        scratch_shapes=[
            pltpu.VMEM((total, 256), F32),
            pltpu.VMEM((512, 256), BF16),
            pltpu.SemaphoreType.DMA((len(blocks),)),
        ],
        compiler_params=pltpu.CompilerParams(vmem_limit_bytes=UPDATE_VMEM),
    )(mine, other, inverse, gram_inverse, *pieces, trailing)


def cross_kernel(initial, halves, blocks, block, chunk, *refs):
    refs = list(refs)
    column, first = whereabouts()
    total = refs.pop(0)[...] if initial else None
    count = 2 if halves else 1
    *pieces, trailing = refs[:-count]
    outs = refs[-count:]
    for piece, row, offset, low in blocks:
        left = split(pieces[piece][row : row + block, :])
        right = split(trailing[rows_at(column, offset, low, chunk, block), :])
        product = contract(
            jnp.concatenate([left[0], left[1], left[0]], axis=0),
            jnp.concatenate([right[0], right[0], right[1]], axis=0),
            ((0,), (0,)),
        )
        total = product if total is None else total + product
    if halves:
        outs[0][...] = jnp.where(first, total[:128, :], total[128:, :])
        outs[1][...] = jnp.where(first, total[128:, :], total[:128, :])
    else:
        outs[0][...] = total


def cross_part(initial, pieces, spots, trailing, halves, block):
    blocks = blocks_of(spots, block)
    vmem = pl.BlockSpec(memory_space=pltpu.VMEM)
    given = [] if initial is None else [initial]
    shapes = [(128, 256)] * 2 if halves else [(256, 256)]
    return pl.pallas_call(
        lambda *refs: cross_kernel(bool(given), halves, blocks, block, trailing.shape[0] // 4, *refs),
        out_shape=[jax.ShapeDtypeStruct(shape, F32) for shape in shapes],
        in_specs=[vmem] * (len(given) + len(pieces) + 1),
        out_specs=[vmem] * len(shapes),
        compiler_params=pltpu.CompilerParams(vmem_limit_bytes=CROSS_VMEM),
    )(*given, *pieces, trailing)


def gram_kernel(panel, keep, send):
    gram = contract(panel[...], panel[...], ((0,), (0,)), HIGHEST)
    one = jnp.concatenate([gram[:128, :128], gram[:64, 128:]], axis=0)
    two = jnp.concatenate([gram[128:, 128:], gram[64:128, 128:]], axis=0)
    _, first = whereabouts()
    keep[...] = jnp.where(first, one, two)
    send[...] = jnp.where(first, two, one)


def gram_part(panel):
    vmem = pl.BlockSpec(memory_space=pltpu.VMEM)
    return pl.pallas_call(
        gram_kernel,
        out_shape=[jax.ShapeDtypeStruct((192, 128), F32)] * 2,
        in_specs=[vmem],
        out_specs=[vmem, vmem],
        compiler_params=pltpu.CompilerParams(vmem_limit_bytes=16 << 20),
    )(panel)


def over_rows(move):
    pairs = []
    for z in range(4):
        for x in range(4):
            for core in range(2):
                z2, x2, core2 = move(z, x, core)
                pairs.append(((z * 4 + x) * 2 + core, (z2 % 4 * 4 + x2 % 4) * 2 + core2))
    return pairs


ORDER = (1, 3, 2)


PARTNER = over_rows(lambda z, x, core: (z, x, 1 - core))
FIRST = [over_rows(lambda z, x, core, k=k: (z, x ^ k, core) if core == 0 else (z ^ k, x, core)) for k in ORDER]
SECOND = [over_rows(lambda z, x, core, k=k: (z ^ k, x, core) if core == 0 else (z, x ^ k, core)) for k in ORDER]


def around(k):
    return [(i, (i + k) % 4) for i in range(4)]


def move(name, part, axis, pairs):
    with jax.named_scope(name):
        return lax.ppermute(part, axis, pairs)


def exchange_sum(name, part, axis, moves):
    others = [move(name, part, axis, pairs) for pairs in moves]
    return (others[0] + others[1]) + (part + others[2])


def partner(name, part):
    return move(name, part, "rows", PARTNER)


def local(panel_cols, trailing):
    rows_total = trailing.shape[0] * lax.axis_size("rows")
    shrink = 1.0 / math.sqrt(rows_total)
    size = panel_cols.shape[0]
    half = size // 2
    barrier = lax.optimization_barrier
    left = move("left", panel_cols, "cols", around(1))
    right = move("right", panel_cols, "cols", around(-1))

    keep, send = gram_part(panel_cols)
    gram = keep + partner("gram_halves", send)
    gram = exchange_sum("gram_first", gram, "rows", FIRST)
    gram = exchange_sum("gram_second", gram, "rows", SECOND)
    left, _ = barrier((left, gram))
    right, _ = barrier((right, gram))
    far1 = move("far1", left[:half], "cols", around(1))
    far2 = move("far2", right[half:], "cols", around(-1))
    gram = exchange_sum("gram_cols", gram, "cols", [around(k) for k in ORDER])
    r_factor, inverse, gram_inverse = factor(gram, partner("gram_join", gram), shrink, 64, 8)

    (cross,) = cross_part(None, (panel_cols, left, right), ((size, 0, 0), (size, 3, 0), (size, 1, 0)), trailing, False, BLOCK)
    (cross,) = cross_part(cross, (far2,), ((half, 2, half),), trailing, False, BLOCK)
    inverse, far1, cross = barrier((inverse, far1, cross))
    keep, send = cross_part(cross, (far1,), ((half, 2, 0),), trailing, True, BLOCK)
    cross = keep + partner("cross_halves", send)
    cross = exchange_sum("cross_first", cross, "rows", FIRST)
    cross = exchange_sum("cross_second", cross, "rows", SECOND)
    pieces = (panel_cols, left, right, far1, far2)
    spots = ((size, 0, 0), (size, 3, 0), (size, 1, 0), (half, 2, 0), (half, 2, half))
    updated, r_cross = update(cross, partner("cross_join", cross), inverse, gram_inverse, pieces, spots, trailing, shrink, 256)
    return (r_factor, r_cross, updated)


def solution(mesh):
    in_specs = (P(("rows", "cols"), None), P("rows", "cols"))
    out_specs = (P(), P(None, "cols"), P("rows", "cols"))
    return jax.shard_map(local, mesh=mesh, in_specs=in_specs, out_specs=out_specs, check_vma=False)
```

```python
import math

import jax
import jax.numpy as jnp
from jax import lax
from jax.experimental import pallas as pl
from jax.experimental.pallas import tpu as pltpu
from jax.sharding import PartitionSpec as P

F32, BF16 = jnp.float32, jnp.bfloat16
HIGHEST = lax.Precision.HIGHEST
BLOCK = 512
FEWER = 64
UPDATE_VMEM = 14 << 20
CROSS_VMEM = 8 << 20

def split(value):
    high = value.astype(BF16)
    return high, (value - high.astype(F32)).astype(BF16)

def contract(left, right, dims, precision=None):
    return lax.dot_general(left, right, (dims, ((), ())), precision=precision, preferred_element_type=F32)

def factor_block(block, group):
    size = block.shape[0]
    lane = lax.broadcasted_iota(jnp.int32, (size, 2 * size), 1)
    row = lax.broadcasted_iota(jnp.int32, (size, 2 * size), 0)
    wide = jnp.concatenate([block, jnp.zeros((size, size), F32)], axis=1)
    wide = jnp.where(lane == row + size, 1.0, wide)
    for first in range(0, size, group):
        columns = [jnp.broadcast_to(wide[:, first + g : first + g + 1], wide.shape) for g in range(group)]
        rows = [wide[first + g : first + g + 1, :] for g in range(group)]
        small = [[columns[j][first + i : first + i + 1, :] for j in range(group)] for i in range(group)]
        change = None
        for g in range(group):
            inv = 1.0 / small[g][g]
            scaled = rows[g] * inv
            for i in range(g + 1, group):
                ratio = small[i][g] * inv
                rows[i] = rows[i] - ratio * rows[g]
                for j in range(g + 1, group):
                    small[i][j] = small[i][j] - ratio * small[g][j]
            for j in range(g + 1, group):
                columns[j] = columns[j] - columns[g] * (small[g][j] * inv)
            term = jnp.where(row > first + g, columns[g] * scaled, 0.0)
            change = term if change is None else change + term
        wide = wide - change
    diagonal = jnp.sum(jnp.where(lane == row, wide, 0.0), axis=1, keepdims=True)
    wide = wide * lax.rsqrt(diagonal)
    return wide

def factor_kernel(shrink, size, group, mine, other, r_factor, inverse, gram_inverse, work):
    _, first = whereabouts()
    one = jnp.where(first, mine[...], other[...])
    two = jnp.where(first, other[...], mine[...])
    work[:128, :128] = one[:128, :]
    work[:64, 128:256] = one[128:, :]
    work[64:128, 128:256] = two[128:, :]
    work[128:, :128] = jnp.zeros((128, 128), F32)
    work[128:, 128:256] = two[:128, :]
    rows = lax.broadcasted_iota(jnp.int32, (256, 256), 0)
    lanes = lax.broadcasted_iota(jnp.int32, (256, 256), 1)
    work[:, 256:] = (rows == lanes).astype(F32)
    for first in range(0, 256, size):
        last = first + size
        both = factor_block(work[first:last, first:last], group)
        done = contract(both[:, size:], work[first:last, :], ((1,), (0,)), HIGHEST)
        work[first:last, :] = done
        if last < 256:
            work[last:, :] -= contract(done[:, last:256], done, ((0,), (0,)), HIGHEST)
    r_factor[...] = jnp.where(rows <= lanes, work[:, :256], 0.0) * shrink
    lower = jnp.where(rows >= lanes, work[:, 256:], 0.0)
    inverse[...] = lower
    gram_inverse[...] = contract(lower, lower, ((0,), (0,)), HIGHEST)

def factor(mine, other, shrink, size=64, group=4):
    full = jax.ShapeDtypeStruct((256, 256), F32)
    return pl.pallas_call(
        lambda *refs: factor_kernel(shrink, size, group, *refs),
        out_shape=[full, full, full],
        in_specs=[pl.BlockSpec(memory_space=pltpu.VMEM)] * 2,
        out_specs=[pl.BlockSpec(memory_space=pltpu.VMEM)] * 3,
        scratch_shapes=[pltpu.VMEM((256, 512), F32)],
        cost_estimate=pl.CostEstimate(flops=8000000000, bytes_accessed=0, transcendentals=0),
        compiler_params=pltpu.CompilerParams(vmem_limit_bytes=16 << 20),
    )(mine, other)

def whereabouts():
    return lax.axis_index("cols"), lax.rem(lax.axis_index("rows"), 2) == 0


def blocks_of(pieces, block):
    return [
        (n, row, offset, low + row, min(block, count - row))
        for n, (count, offset, low) in enumerate(pieces)
        for row in range(0, count, block)
    ]


def rows_at(column, offset, low, chunk, count):
    return pl.ds(pl.multiple_of(lax.rem(column + offset, 4) * chunk + low, 64), count)


def update_kernel(shrink, blocks, chunk, mine, other, inverse, gram_inverse, *refs):
    *pieces, trailing, updated, r_cross, result, weights, sems = refs
    column, first = whereabouts()
    top = jnp.where(first, mine[...], other[...])
    bottom = jnp.where(first, other[...], mine[...])
    cross = jnp.concatenate([top, bottom], axis=0)
    weights[:256, :], weights[256:, :] = split(contract(gram_inverse[...], cross, ((1,), (0,)), HIGHEST))
    stores, done = [], 0
    for n, (piece, row, offset, low_row, count) in enumerate(blocks):
        rows = rows_at(column, offset, low_row, chunk, count)
        high, low = split(pieces[piece][row : row + count, :])
        product = contract(high, weights[:256, :], ((1,), (0,)))
        product += contract(low, weights[:256, :], ((1,), (0,)))
        product += contract(high, weights[256:, :], ((1,), (0,)))
        here = pl.ds(done, count)
        done += count
        result[here, :] = trailing[rows, :] - product
        store = pltpu.make_async_copy(result.at[here], updated.at[rows], sems.at[n])
        store.start()
        stores.append(store)
    r_cross[...] = contract(inverse[...], cross, ((1,), (0,)), HIGHEST) * shrink
    for store in stores:
        store.wait()


def update(mine, other, inverse, gram_inverse, pieces, spots, trailing, shrink, block):
    blocks = blocks_of(spots, block)
    vmem, anywhere = pl.BlockSpec(memory_space=pltpu.VMEM), pl.BlockSpec(memory_space=pl.ANY)
    total = trailing.shape[0]
    return pl.pallas_call(
        lambda *refs: update_kernel(shrink, blocks, total // 4, *refs),
        out_shape=[jax.ShapeDtypeStruct(trailing.shape, F32), jax.ShapeDtypeStruct((256, 256), F32)],
        in_specs=[vmem] * (len(pieces) + 5),
        out_specs=[anywhere, vmem],
        scratch_shapes=[
            pltpu.VMEM((total, 256), F32),
            pltpu.VMEM((512, 256), BF16),
            pltpu.SemaphoreType.DMA((len(blocks),)),
        ],
        compiler_params=pltpu.CompilerParams(vmem_limit_bytes=UPDATE_VMEM),
    )(mine, other, inverse, gram_inverse, *pieces, trailing)


def cross_kernel(initial, halves, blocks, chunk, *refs):
    refs = list(refs)
    column, first = whereabouts()
    total = refs.pop(0)[...] if initial else None
    count = 2 if halves else 1
    *pieces, trailing = refs[:-count]
    outs = refs[-count:]
    for piece, row, offset, low, size in blocks:
        left = split(pieces[piece][row : row + size, :])
        right = split(trailing[rows_at(column, offset, low, chunk, size), :])
        product = contract(
            jnp.concatenate([left[0], left[1], left[0]], axis=0),
            jnp.concatenate([right[0], right[0], right[1]], axis=0),
            ((0,), (0,)),
        )
        total = product if total is None else total + product
    if halves:
        outs[0][...] = jnp.where(first, total[:128, :], total[128:, :])
        outs[1][...] = jnp.where(first, total[128:, :], total[:128, :])
    else:
        outs[0][...] = total


def cross_part(initial, pieces, spots, trailing, halves, block):
    blocks = blocks_of(spots, block)
    vmem = pl.BlockSpec(memory_space=pltpu.VMEM)
    given = [] if initial is None else [initial]
    shapes = [(128, 256)] * 2 if halves else [(256, 256)]
    return pl.pallas_call(
        lambda *refs: cross_kernel(bool(given), halves, blocks, trailing.shape[0] // 4, *refs),
        out_shape=[jax.ShapeDtypeStruct(shape, F32) for shape in shapes],
        in_specs=[vmem] * (len(given) + len(pieces) + 1),
        out_specs=[vmem] * len(shapes),
        compiler_params=pltpu.CompilerParams(vmem_limit_bytes=CROSS_VMEM),
    )(*given, *pieces, trailing)


def gram_kernel(panel, keep, send):
    gram = contract(panel[...], panel[...], ((0,), (0,)), HIGHEST)
    one = jnp.concatenate([gram[:128, :128], gram[:64, 128:]], axis=0)
    two = jnp.concatenate([gram[128:, 128:], gram[64:128, 128:]], axis=0)
    _, first = whereabouts()
    keep[...] = jnp.where(first, one, two)
    send[...] = jnp.where(first, two, one)


def gram_part(panel):
    vmem = pl.BlockSpec(memory_space=pltpu.VMEM)
    return pl.pallas_call(
        gram_kernel,
        out_shape=[jax.ShapeDtypeStruct((192, 128), F32)] * 2,
        in_specs=[vmem],
        out_specs=[vmem, vmem],
        compiler_params=pltpu.CompilerParams(vmem_limit_bytes=16 << 20),
    )(panel)


def over_rows(move):
    pairs = []
    for z in range(4):
        for x in range(4):
            for core in range(2):
                z2, x2, core2 = move(z, x, core)
                pairs.append(((z * 4 + x) * 2 + core, (z2 % 4 * 4 + x2 % 4) * 2 + core2))
    return pairs


ORDER = (1, 3, 2)


PARTNER = over_rows(lambda z, x, core: (z, x, 1 - core))
FIRST = [over_rows(lambda z, x, core, k=k: (z, x ^ k, core) if core == 0 else (z ^ k, x, core)) for k in ORDER]
SECOND = [over_rows(lambda z, x, core, k=k: (z ^ k, x, core) if core == 0 else (z, x ^ k, core)) for k in ORDER]


def around(k):
    return [(i, (i + k) % 4) for i in range(4)]


def move(name, part, axis, pairs):
    with jax.named_scope(name):
        return lax.ppermute(part, axis, pairs)


def exchange_sum(name, part, axis, moves):
    others = [move(name, part, axis, pairs) for pairs in moves]
    return (others[0] + others[1]) + (part + others[2])


def partner(name, part):
    return move(name, part, "rows", PARTNER)


def local(panel_cols, trailing):
    rows_total = trailing.shape[0] * lax.axis_size("rows")
    shrink = 1.0 / math.sqrt(rows_total)
    size = panel_cols.shape[0]
    half = size // 2
    fewer = half - FEWER
    barrier = lax.optimization_barrier
    left = move("left", panel_cols, "cols", around(1))
    right = move("right", panel_cols, "cols", around(-1))

    keep, send = gram_part(panel_cols)
    gram = keep + partner("gram_halves", send)
    gram = exchange_sum("gram_first", gram, "rows", FIRST)
    gram = exchange_sum("gram_second", gram, "rows", SECOND)
    left, _ = barrier((left, gram))
    right, _ = barrier((right, gram))
    far1 = move("far1", left[:fewer], "cols", around(1))
    far2 = move("far2", right[fewer:], "cols", around(-1))
    gram = exchange_sum("gram_cols", gram, "cols", [around(k) for k in ORDER])
    r_factor, inverse, gram_inverse = factor(gram, partner("gram_join", gram), shrink, 64, 8)

    (cross,) = cross_part(None, (panel_cols, left, right), ((size, 0, 0), (size, 3, 0), (size, 1, 0)), trailing, False, BLOCK)
    (cross,) = cross_part(cross, (far2,), ((size - fewer, 2, fewer),), trailing, False, BLOCK)
    inverse, far1, cross = barrier((inverse, far1, cross))
    keep, send = cross_part(cross, (far1,), ((fewer, 2, 0),), trailing, True, BLOCK)
    cross = keep + partner("cross_halves", send)
    cross = exchange_sum("cross_first", cross, "rows", FIRST)
    cross = exchange_sum("cross_second", cross, "rows", SECOND)
    pieces = (panel_cols, left, right, far1, far2)
    spots = ((size, 0, 0), (size, 3, 0), (size, 1, 0), (fewer, 2, 0), (size - fewer, 2, fewer))
    updated, r_cross = update(cross, partner("cross_join", cross), inverse, gram_inverse, pieces, spots, trailing, shrink, 256)
    return (r_factor, r_cross, updated)


def solution(mesh):
    in_specs = (P(("rows", "cols"), None), P("rows", "cols"))
    out_specs = (P(), P(None, "cols"), P("rows", "cols"))
    return jax.shard_map(local, mesh=mesh, in_specs=in_specs, out_specs=out_specs, check_vma=False)
```

```python
import math

import jax
import jax.numpy as jnp
from jax import lax
from jax.experimental import pallas as pl
from jax.experimental.pallas import tpu as pltpu
from jax.sharding import PartitionSpec as P

F32, BF16 = jnp.float32, jnp.bfloat16
HIGHEST = lax.Precision.HIGHEST
BLOCK = 512
FEWER = 64
UPDATE_VMEM = 14 << 20
CROSS_VMEM = 8 << 20

def split(value):
    high = value.astype(BF16)
    return high, (value - high.astype(F32)).astype(BF16)

def contract(left, right, dims, precision=None):
    return lax.dot_general(left, right, (dims, ((), ())), precision=precision, preferred_element_type=F32)

def factor_block(block, group):
    size = block.shape[0]
    lane = lax.broadcasted_iota(jnp.int32, (size, 2 * size), 1)
    row = lax.broadcasted_iota(jnp.int32, (size, 2 * size), 0)
    wide = jnp.concatenate([block, jnp.zeros((size, size), F32)], axis=1)
    wide = jnp.where(lane == row + size, 1.0, wide)
    for first in range(0, size, group):
        columns = [jnp.broadcast_to(wide[:, first + g : first + g + 1], wide.shape) for g in range(group)]
        rows = [wide[first + g : first + g + 1, :] for g in range(group)]
        small = [[columns[j][first + i : first + i + 1, :] for j in range(group)] for i in range(group)]
        change = None
        for g in range(group):
            inv = 1.0 / small[g][g]
            scaled = rows[g] * inv
            for i in range(g + 1, group):
                ratio = small[i][g] * inv
                rows[i] = rows[i] - ratio * rows[g]
                for j in range(g + 1, group):
                    small[i][j] = small[i][j] - ratio * small[g][j]
            for j in range(g + 1, group):
                columns[j] = columns[j] - columns[g] * (small[g][j] * inv)
            term = jnp.where(row > first + g, columns[g] * scaled, 0.0)
            change = term if change is None else change + term
        wide = wide - change
    diagonal = jnp.sum(jnp.where(lane == row, wide, 0.0), axis=1, keepdims=True)
    wide = wide * lax.rsqrt(diagonal)
    return wide

def factor_kernel(shrink, size, group, mine, other, r_factor, inverse, gram_inverse, work):
    _, first = whereabouts()
    one = jnp.where(first, mine[...], other[...])
    two = jnp.where(first, other[...], mine[...])
    work[:128, :128] = one[:128, :]
    work[:64, 128:256] = one[128:, :]
    work[64:128, 128:256] = two[128:, :]
    work[128:, :128] = jnp.zeros((128, 128), F32)
    work[128:, 128:256] = two[:128, :]
    rows = lax.broadcasted_iota(jnp.int32, (256, 256), 0)
    lanes = lax.broadcasted_iota(jnp.int32, (256, 256), 1)
    work[:, 256:] = (rows == lanes).astype(F32)
    for first in range(0, 256, size):
        last = first + size
        both = factor_block(work[first:last, first:last], group)
        done = contract(both[:, size:], work[first:last, :], ((1,), (0,)), HIGHEST)
        work[first:last, :] = done
        if last < 256:
            work[last:, :] -= contract(done[:, last:256], done, ((0,), (0,)), HIGHEST)
    r_factor[...] = jnp.where(rows <= lanes, work[:, :256], 0.0) * shrink
    lower = jnp.where(rows >= lanes, work[:, 256:], 0.0)
    inverse[...] = lower
    gram_inverse[...] = contract(lower, lower, ((0,), (0,)), HIGHEST)

def factor(mine, other, shrink, size=64, group=4):
    full = jax.ShapeDtypeStruct((256, 256), F32)
    return pl.pallas_call(
        lambda *refs: factor_kernel(shrink, size, group, *refs),
        out_shape=[full, full, full],
        in_specs=[pl.BlockSpec(memory_space=pltpu.VMEM)] * 2,
        out_specs=[pl.BlockSpec(memory_space=pltpu.VMEM)] * 3,
        scratch_shapes=[pltpu.VMEM((256, 512), F32)],
        cost_estimate=pl.CostEstimate(flops=8000000000, bytes_accessed=0, transcendentals=0),
        compiler_params=pltpu.CompilerParams(vmem_limit_bytes=16 << 20),
    )(mine, other)

def whereabouts():
    return lax.axis_index("cols"), lax.rem(lax.axis_index("rows"), 2) == 0


def blocks_of(pieces, block):
    return [
        (n, row, offset, low + row, min(block, count - row))
        for n, (count, offset, low) in enumerate(pieces)
        for row in range(0, count, block)
    ]


def rows_at(column, offset, low, chunk, count):
    return pl.ds(pl.multiple_of(lax.rem(column + offset, 4) * chunk + low, 64), count)


def times(square, half, top):
    columns = jnp.where(top, square[:, :128], square[:, 128:])
    return contract(columns, half[...], ((1,), (0,)), HIGHEST)


def begin_kernel(mine, inverse, gram_inverse, weights_mine, coupling_mine):
    _, first = whereabouts()
    weights_mine[...] = times(gram_inverse, mine, first)
    coupling_mine[...] = times(inverse, mine, first)


def begin(mine, inverse, gram_inverse):
    vmem = pl.BlockSpec(memory_space=pltpu.VMEM)
    return pl.pallas_call(
        begin_kernel,
        out_shape=[jax.ShapeDtypeStruct((256, 256), F32)] * 2,
        in_specs=[vmem] * 3,
        out_specs=[vmem] * 2,
        compiler_params=pltpu.CompilerParams(vmem_limit_bytes=CROSS_VMEM),
    )(mine, inverse, gram_inverse)


def update_kernel(shrink, blocks, chunk, weights_mine, coupling_mine, other, inverse, gram_inverse, *refs):
    *pieces, trailing, updated, r_cross, result, weights, sems = refs
    column, first = whereabouts()
    full = weights_mine[...] + times(gram_inverse, other, ~first)
    weights[:256, :], weights[256:, :] = split(full)
    stores, done = [], 0
    for n, (piece, row, offset, low_row, count) in enumerate(blocks):
        rows = rows_at(column, offset, low_row, chunk, count)
        high, low = split(pieces[piece][row : row + count, :])
        product = contract(high, weights[:256, :], ((1,), (0,)))
        product += contract(low, weights[:256, :], ((1,), (0,)))
        product += contract(high, weights[256:, :], ((1,), (0,)))
        here = pl.ds(done, count)
        done += count
        result[here, :] = trailing[rows, :] - product
        store = pltpu.make_async_copy(result.at[here], updated.at[rows], sems.at[n])
        store.start()
        stores.append(store)
    r_cross[...] = (coupling_mine[...] + times(inverse, other, ~first)) * shrink
    for store in stores:
        store.wait()


def update(begun, other, inverse, gram_inverse, pieces, spots, trailing, shrink, block):
    blocks = blocks_of(spots, block)
    vmem, anywhere = pl.BlockSpec(memory_space=pltpu.VMEM), pl.BlockSpec(memory_space=pl.ANY)
    total = trailing.shape[0]
    return pl.pallas_call(
        lambda *refs: update_kernel(shrink, blocks, total // 4, *refs),
        out_shape=[jax.ShapeDtypeStruct(trailing.shape, F32), jax.ShapeDtypeStruct((256, 256), F32)],
        in_specs=[vmem] * (len(pieces) + 6),
        out_specs=[anywhere, vmem],
        scratch_shapes=[
            pltpu.VMEM((total, 256), F32),
            pltpu.VMEM((512, 256), BF16),
            pltpu.SemaphoreType.DMA((len(blocks),)),
        ],
        compiler_params=pltpu.CompilerParams(vmem_limit_bytes=UPDATE_VMEM),
    )(*begun, other, inverse, gram_inverse, *pieces, trailing)


def cross_kernel(initial, halves, blocks, chunk, *refs):
    refs = list(refs)
    column, first = whereabouts()
    total = refs.pop(0)[...] if initial else None
    count = 2 if halves else 1
    *pieces, trailing = refs[:-count]
    outs = refs[-count:]
    for piece, row, offset, low, size in blocks:
        left = split(pieces[piece][row : row + size, :])
        right = split(trailing[rows_at(column, offset, low, chunk, size), :])
        product = contract(
            jnp.concatenate([left[0], left[1], left[0]], axis=0),
            jnp.concatenate([right[0], right[0], right[1]], axis=0),
            ((0,), (0,)),
        )
        total = product if total is None else total + product
    if halves:
        outs[0][...] = jnp.where(first, total[:128, :], total[128:, :])
        outs[1][...] = jnp.where(first, total[128:, :], total[:128, :])
    else:
        outs[0][...] = total


def cross_part(initial, pieces, spots, trailing, halves, block):
    blocks = blocks_of(spots, block)
    vmem = pl.BlockSpec(memory_space=pltpu.VMEM)
    given = [] if initial is None else [initial]
    shapes = [(128, 256)] * 2 if halves else [(256, 256)]
    return pl.pallas_call(
        lambda *refs: cross_kernel(bool(given), halves, blocks, trailing.shape[0] // 4, *refs),
        out_shape=[jax.ShapeDtypeStruct(shape, F32) for shape in shapes],
        in_specs=[vmem] * (len(given) + len(pieces) + 1),
        out_specs=[vmem] * len(shapes),
        compiler_params=pltpu.CompilerParams(vmem_limit_bytes=CROSS_VMEM),
    )(*given, *pieces, trailing)


def gram_kernel(panel, keep, send):
    gram = contract(panel[...], panel[...], ((0,), (0,)), HIGHEST)
    one = jnp.concatenate([gram[:128, :128], gram[:64, 128:]], axis=0)
    two = jnp.concatenate([gram[128:, 128:], gram[64:128, 128:]], axis=0)
    _, first = whereabouts()
    keep[...] = jnp.where(first, one, two)
    send[...] = jnp.where(first, two, one)


def gram_part(panel):
    vmem = pl.BlockSpec(memory_space=pltpu.VMEM)
    return pl.pallas_call(
        gram_kernel,
        out_shape=[jax.ShapeDtypeStruct((192, 128), F32)] * 2,
        in_specs=[vmem],
        out_specs=[vmem, vmem],
        compiler_params=pltpu.CompilerParams(vmem_limit_bytes=16 << 20),
    )(panel)


def over_rows(move):
    pairs = []
    for z in range(4):
        for x in range(4):
            for core in range(2):
                z2, x2, core2 = move(z, x, core)
                pairs.append(((z * 4 + x) * 2 + core, (z2 % 4 * 4 + x2 % 4) * 2 + core2))
    return pairs


ORDER = (1, 3, 2)


PARTNER = over_rows(lambda z, x, core: (z, x, 1 - core))
FIRST = [over_rows(lambda z, x, core, k=k: (z, x ^ k, core) if core == 0 else (z ^ k, x, core)) for k in ORDER]
SECOND = [over_rows(lambda z, x, core, k=k: (z ^ k, x, core) if core == 0 else (z, x ^ k, core)) for k in ORDER]


def around(k):
    return [(i, (i + k) % 4) for i in range(4)]


def move(name, part, axis, pairs):
    with jax.named_scope(name):
        return lax.ppermute(part, axis, pairs)


def exchange_sum(name, part, axis, moves):
    others = [move(name, part, axis, pairs) for pairs in moves]
    return (others[0] + others[1]) + (part + others[2])


def partner(name, part):
    return move(name, part, "rows", PARTNER)


def local(panel_cols, trailing):
    rows_total = trailing.shape[0] * lax.axis_size("rows")
    shrink = 1.0 / math.sqrt(rows_total)
    size = panel_cols.shape[0]
    half = size // 2
    fewer = half - FEWER
    barrier = lax.optimization_barrier
    left = move("left", panel_cols, "cols", around(1))
    right = move("right", panel_cols, "cols", around(-1))

    keep, send = gram_part(panel_cols)
    gram = keep + partner("gram_halves", send)
    gram = exchange_sum("gram_first", gram, "rows", FIRST)
    gram = exchange_sum("gram_second", gram, "rows", SECOND)
    left, _ = barrier((left, gram))
    right, _ = barrier((right, gram))
    far1 = move("far1", left[:fewer], "cols", around(1))
    far2 = move("far2", right[fewer:], "cols", around(-1))
    gram = exchange_sum("gram_cols", gram, "cols", [around(k) for k in ORDER])
    r_factor, inverse, gram_inverse = factor(gram, partner("gram_join", gram), shrink, 64, 8)

    (cross,) = cross_part(None, (panel_cols, left, right), ((size, 0, 0), (size, 3, 0), (size, 1, 0)), trailing, False, BLOCK)
    (cross,) = cross_part(cross, (far2,), ((size - fewer, 2, fewer),), trailing, False, BLOCK)
    inverse, far1, cross = barrier((inverse, far1, cross))
    keep, send = cross_part(cross, (far1,), ((fewer, 2, 0),), trailing, True, BLOCK)
    cross = keep + partner("cross_halves", send)
    cross = exchange_sum("cross_first", cross, "rows", FIRST)
    cross = exchange_sum("cross_second", cross, "rows", SECOND)
    pieces = (panel_cols, left, right, far1, far2)
    spots = ((size, 0, 0), (size, 3, 0), (size, 1, 0), (fewer, 2, 0), (size - fewer, 2, fewer))
    updated, r_cross = update(begin(cross, inverse, gram_inverse), partner("cross_join", cross), inverse, gram_inverse, pieces, spots, trailing, shrink, 256)
    return (r_factor, r_cross, updated)


def solution(mesh):
    in_specs = (P(("rows", "cols"), None), P("rows", "cols"))
    out_specs = (P(), P(None, "cols"), P("rows", "cols"))
    return jax.shard_map(local, mesh=mesh, in_specs=in_specs, out_specs=out_specs, check_vma=False)
```
